128 devices in a mesh: row: 8 (over z, core), col: 16 (over x, y).
Axes of the slice: x: 4, y: 4, z: 4, core: 2. Of those that a mesh axis runs over, the one named last changes fastest.
Arguments:
- front_panel: float32 [40960, 512], P('row', 'col'), may hold values from -16 to 48, as said below
- front_slab: float32 [40960, 8192], P('row', 'col'), may hold values from -6 to 6
- child_one: bfloat16 [8192, 8192], P('col', 'row'), may hold values from -6 to 6
- child_two: bfloat16 [8192, 8192], P('col', 'row'), may hold values from -6 to 6
- map_one: int32 [32], replicated, may hold values from 0 to 159, as said below
- map_two: int32 [32], replicated, may hold values from 0 to 159, as said below
Outputs:
- factor_panel: float32 [40960, 512], P('row', 'col')
- slab_out: float32 [40960, 8192], P('row', 'col')
The draws below stay inside these ranges and needn't reach their ends.
Inputs may be any that keep to these rules, and one draw needn't show every extreme that they name: `front_panel`: its first 512 rows are, in all 512 columns, a symmetric positive definite block. `map_one`: distinct root row blocks. Of the 20 blocks of one index of row (numbers k * 20 to (k + 1) * 20 - 1) at most 8 are named, and exactly 8 for some index of row. `map_two`: as map_one, drawn independently.
All inputs are finite; a program needn't handle non-finite values.
Results may differ from the reference program's by a relative error of at most 0.0003.
Values may be sent and summed in bfloat16 or wider, within the bound.
A program may use at most 192 MiB of HBM per device.

```python
import jax
import jax.numpy as jnp
from jax import lax

P_SIZE = 256
SLAB = 8192
BLK = 256
M = 40960
CRB = 32
CR = 8192
RB = 20
OWNERS = 8
CAPB = 8
N_ROW = 8
N_COL = 16


def draw_front_panel(key, part):
    width = 2 * P_SIZE
    keys = jax.random.split(key, 2)
    base = jax.random.normal(keys[0], (width, width), jnp.float32)
    below = jnp.clip(jax.random.normal(keys[1], (M - width, width), jnp.float32), -6.0, 6.0)
    gram = jnp.dot(base, base.T, precision=lax.Precision.HIGHEST) / width
    gram = 0.5 * (gram + gram.T)
    top = 8.0 * (gram + jnp.eye(width, dtype=jnp.float32))
    return jnp.concatenate([top, below], 0).astype(jnp.float32)


def routed_blocks(key):
    keys = jax.random.split(key, 4)
    busiest = jax.random.randint(keys[0], (), 0, OWNERS)
    owner_keys = jax.random.split(keys[1], OWNERS)
    picks = jax.vmap(lambda single: jax.random.permutation(single, RB)[:CAPB])(owner_keys)
    owners = jnp.arange(OWNERS, dtype=jnp.int32)[:, None]
    blocks = (owners * RB + picks.astype(jnp.int32)).reshape(-1)
    owner_flat = jnp.broadcast_to(owners, (OWNERS, CAPB)).reshape(-1)
    order = jax.random.permutation(keys[2], OWNERS * CAPB).astype(jnp.int32)
    score = jnp.where(owner_flat == busiest, 0, order + 1)
    chosen = blocks[jnp.argsort(score, stable=True)[:CRB]]
    return chosen[jax.random.permutation(keys[3], CRB)].astype(jnp.int32)


def draw_map_one(key, part):
    return routed_blocks(jax.random.fold_in(key, 11))


def draw_map_two(key, part):
    return routed_blocks(jax.random.fold_in(key, 23))


def levels(rng, extent, pieces, least, top_value):
    loudness = 1.0
    for position, parts in pieces:
        steps = jax.random.uniform(jax.random.fold_in(jax.random.fold_in(rng, 6), position), (parts,), jnp.float32, least / len(pieces), top_value / len(pieces))
        loudness = loudness * jnp.repeat(jnp.exp(steps), extent[position] // parts).reshape((-1,) + (1,) * (len(extent) - 1 - position))
    return loudness


def noise(key, dims, deviation, limit, cuts=(), kind=jnp.bfloat16):
    result = deviation * jax.random.normal(key, dims, jnp.float32)
    if cuts:
        result = result * levels(key, dims, cuts, -0.22, 0.18)
    return jnp.clip(result, -limit, limit).astype(kind)


def setup_inputs(seed: int = 0) -> dict:
    splits = jax.random.split(jax.random.key(seed), 7)
    front_panel = draw_front_panel(jax.random.fold_in(splits[6], 71), 0)
    front_slab = noise(splits[1], (M, SLAB), 1.0, 6.0, ((0, 8), (1, 16)), jnp.float32)
    child_one = noise(splits[2], (CR, SLAB), 1.0, 6.0, ((0, 16), (1, 8)))
    child_two = noise(splits[3], (CR, SLAB), 1.0, 6.0, ((0, 16), (1, 8)))
    map_one = draw_map_one(jax.random.fold_in(splits[6], 71), 0)
    map_two = draw_map_two(jax.random.fold_in(splits[6], 71), 0)
    return dict(front_panel=front_panel, front_slab=front_slab, child_one=child_one, child_two=child_two, map_one=map_one, map_two=map_two)


def extend(slab, child, mapping):
    piece = SLAB // (N_ROW * N_COL)
    moved = child.astype(jnp.float32).reshape(CR, N_ROW, N_COL, piece)
    moved = jnp.transpose(moved, (0, 2, 1, 3)).reshape(CR, SLAB)
    target = (mapping[:, None] * BLK + jnp.arange(BLK, dtype=jnp.int32)[None, :]).reshape(-1).astype(jnp.int32)
    return slab.at[target].add(moved)

def inverse_factor(block):
    lower = jnp.linalg.cholesky(block)
    identity = jnp.eye(P_SIZE, dtype=jnp.float32)
    return jax.scipy.linalg.solve_triangular(lower, identity, lower=True)

def reference(front_panel, front_slab, child_one, child_two, map_one, map_two):
    highest = lax.Precision.HIGHEST
    assembled = extend(extend(front_slab, child_one, map_one), child_two, map_two)
    inverse_one = inverse_factor(front_panel[:P_SIZE, :P_SIZE])
    first_cols = jnp.dot(front_panel[:, :P_SIZE].astype(jnp.float32), inverse_one.T.astype(jnp.float32), precision=highest, preferred_element_type=jnp.float32)
    second_in = front_panel[:, P_SIZE:] - jnp.dot(first_cols.astype(jnp.float32), first_cols[P_SIZE:2 * P_SIZE].T.astype(jnp.float32), precision=highest, preferred_element_type=jnp.float32)
    inverse_two = inverse_factor(second_in[P_SIZE:2 * P_SIZE])
    second_cols = jnp.dot(second_in.astype(jnp.float32), inverse_two.T.astype(jnp.float32), precision=highest, preferred_element_type=jnp.float32)
    factor_panel = jnp.concatenate([first_cols, second_cols], 1)
    keep = (jnp.arange(M, dtype=jnp.int32) >= 2 * P_SIZE)[:, None]
    masked = jnp.where(keep, factor_panel, jnp.zeros_like(factor_panel))
    slab_rows = factor_panel[2 * P_SIZE:2 * P_SIZE + SLAB]
    slab_out = assembled - jnp.dot(masked.astype(jnp.float32), slab_rows.T.astype(jnp.float32), precision=highest, preferred_element_type=jnp.float32)
    return (factor_panel, slab_out)
```

```python
import functools

import jax
import jax.numpy as jnp
from jax import lax
from jax.experimental import pallas as pl
from jax.experimental.pallas import tpu as pltpu
from jax.sharding import PartitionSpec as P

BLK = 256
PANEL = 512
NC = 16
NR = 8
STRIP = 32
ROWS = 5120
HALF = ROWS // 2
WIDTH = 512
CAP = 8
NS = 2
SUB = BLK // NS
MESH = pl.DeviceIdType.MESH
F32 = jnp.float32
BF16 = jnp.bfloat16
HIGHEST = lax.Precision.HIGHEST


def swap_halves(v):
    return jnp.concatenate([v[:, 64:], v[:, :64]], axis=1)


def exchange_kernel(
    slots, panel, child_one, child_two,
    top, rows_ps, code, scale, arrived,
    pack, got, blocks, outgoing, coded, scales,
    top_send, top_recv, topz_recv, c1_send, c1_recv, c2_send, c2_recv,
    g_send, g_recv, s_send, s_recv, ps_send, ps_recv, psb_send, psb_recv,
):
    row = lax.axis_index("row")
    col = lax.axis_index("col")
    z, core = row // 2, row % 2
    x, y = col // 4, col % 4
    other = z * 2 + (1 - core)

    def at_col(dx, dy):
        return ((x + dx) % 4) * 4 + (y + dy) % 4

    def at_row(dz, dk):
        return ((z + dz) % 4) * 2 + (core + dk) % 2

    plane = [(dx, dy) for dx in range(4) for dy in range(4)]
    away = [d for d in plane if d != (0, 0)]
    line = [(dz, dk) for dz in range(4) for dk in range(2)]
    line_away = [d for d in line if d != (0, 0)]

    barrier = pltpu.get_barrier_semaphore()
    for d in away:
        pl.semaphore_signal(barrier, inc=1, device_id=(row, at_col(*d)), device_id_type=MESH)
    for d in plane:
        pl.semaphore_signal(barrier, inc=1, device_id=(other, at_col(*d)), device_id_type=MESH)
    for dz in range(1, 4):
        for dk in range(2):
            pl.semaphore_signal(barrier, inc=1, device_id=(at_row(dz, dk), col), device_id_type=MESH)
    pl.semaphore_wait(barrier, 37)

    sends = []

    def remote(src, dst, send, recv, to_row, to_col):
        return pltpu.make_async_remote_copy(
            src_ref=src, dst_ref=dst, send_sem=send, recv_sem=recv,
            device_id=(to_row, to_col), device_id_type=MESH,
        )

    def push(*args):
        copy = remote(*args)
        copy.start()
        sends.append(copy)

    def landed(ref, sem):
        pltpu.make_async_copy(ref, ref, sem).wait()

    mine = pl.ds(pl.multiple_of(col * STRIP, STRIP), STRIP)
    strip = panel.at[:, pl.ds(0, PANEL)]

    @pl.when(row == 0)
    def _():
        for n, d in enumerate(line_away):
            remote(strip, top.at[mine], top_send.at[n], topz_recv, at_row(*d), col).start()
        pltpu.make_async_copy(strip, top.at[mine], topz_recv).start()

    landed(top.at[mine], topz_recv)
    for n, d in enumerate(away):
        push(top.at[mine], top.at[mine], top_send.at[7 + n], top_recv.at[col], row, at_col(*d))

    low = lax.broadcasted_iota(jnp.int32, (SUB, 128), 1) < 64
    for s in range(NS):
        for t, child in enumerate((child_one, child_two)):
            for p in range(NC // 2):
                lanes = slice(128 * p, 128 * p + 128)
                first = child[s * SUB:(s + 1) * SUB, lanes]
                second = child[BLK + s * SUB:BLK + (s + 1) * SUB, lanes]
                pack[s, t, 2 * p] = jnp.where(low, first, swap_halves(second))
                pack[s, t, 2 * p + 1] = jnp.where(low, swap_halves(first), second)
        for n, d in enumerate(plane):
            for dk in range(2):
                to = (core + dk) % 2
                src = pack.at[s, to, at_col(*d)]
                dst = got.at[s, col, core]
                if d == (0, 0) and dk == 0:
                    pltpu.make_async_copy(src, dst, c1_recv.at[s, col, core]).start()
                else:
                    push(src, dst, c1_send.at[s, n, dk], c1_recv.at[s, col, core], z * 2 + to, at_col(*d))

    for v in range(9):
        for g in range(2):
            if v + 9 * g < NC:
                to_col = v + 9 * g
                src = panel.at[:, pl.ds(PANEL * (v + 1 - g), PANEL)]

                @pl.when((row == g) & (col != to_col))
                def _():
                    remote(src, rows_ps.at[mine], ps_send.at[v], ps_recv.at[col], row, to_col).start()

                @pl.when((row == g) & (col == to_col))
                def _():
                    pltpu.make_async_copy(src, rows_ps.at[mine], ps_recv.at[col]).start()

    for j in range(ROWS // 128):
        lanes = slice(128 * j, 128 * j + 128)
        v = panel[:, lanes]
        most = jnp.maximum(jnp.max(jnp.abs(v), axis=0, keepdims=True), 1e-30)
        step = most * (1.0 / 32760.0)
        coded[:, lanes] = jnp.round(v * (1.0 / step)).astype(jnp.int32).astype(jnp.int16)
        scales[j:j + 1, :] = step
    pltpu.make_async_copy(scales, scale.at[col], s_recv.at[col]).start()
    for n, d in enumerate(away):
        push(scales, scale.at[col], s_send.at[n], s_recv.at[col], row, at_col(*d))
    halves = [pl.ds(0, HALF), pl.ds(HALF, HALF)]
    for h in range(2):
        pltpu.make_async_copy(coded.at[:, halves[h]], code.at[mine, halves[h]], g_recv.at[h, col]).start()
        for n in range(1, 4):
            d = (n, 0) if h == 0 else (0, n)
            push(coded.at[:, halves[h]], code.at[mine, halves[h]], g_send.at[h, n - 1], g_recv.at[h, col], row, at_col(*d))

    def second_hop(n):
        for h in range(2):
            d = (n, 0) if h == 0 else (0, n)
            source = at_col(*d)
            part = code.at[pl.ds(pl.multiple_of(source * STRIP, STRIP), STRIP), halves[h]]
            landed(part, g_recv.at[h, source])
            for m in range(1, 4):
                to = at_col(0, m) if h == 0 else at_col(m, 0)
                push(part, part, g_send.at[h, 3 + 3 * n + m - 1], g_recv.at[h, source], row, to)

    def rows_hop(s):
        for d in plane:
            for dk in range(2):
                source, k = at_col(*d), (core + dk) % 2
                landed(got.at[s, source, k], c1_recv.at[s, source, k])
        for c in range(NC):
            first = got[s, c, 0]
            second = got[s, c, 1]
            blocks[s, 2 * c] = jnp.where(low, first, swap_halves(second))
            blocks[s, 2 * c + 1] = jnp.where(low, swap_halves(first), second)
        for n, d in enumerate(line):
            to = at_row(*d)
            for q in range(CAP):
                outgoing[s, to, q] = blocks[s, slots[core * NR * CAP + to * CAP + q]]
            dst = arrived.at[core, z, s]
            if d == (0, 0):
                pltpu.make_async_copy(outgoing.at[s, to], dst, c2_recv.at[s, z, core]).start()
            else:
                push(outgoing.at[s, to], dst, c2_send.at[s, n], c2_recv.at[s, z, core], to, col)

    rows_hop(0)
    for n in range(4):
        second_hop(n)
    rows_hop(1)

    root = jnp.where(col < 9, 0, 1)

    @pl.when(row == root)
    def _():
        for d in plane:
            source = at_col(*d)
            landed(rows_ps.at[pl.ds(pl.multiple_of(source * STRIP, STRIP), STRIP)], ps_recv.at[source])
        for n, d in enumerate(((1, 0), (3, 0), (2, 0), (0, 1))):
            remote(rows_ps, rows_ps, psb_send.at[n], psb_recv, at_row(*d), col).start()
        for n, d in enumerate(((1, 0), (3, 0), (2, 0), (0, 1))):
            remote(rows_ps, rows_ps, psb_send.at[n], psb_recv, at_row(*d), col).wait_send()

    @pl.when(row != root)
    def _():
        landed(rows_ps, psb_recv)

    @pl.when((core == root) & (z > 0))
    def _():
        remote(rows_ps, rows_ps, psb_send.at[3], psb_recv, other, col).start()
        remote(rows_ps, rows_ps, psb_send.at[3], psb_recv, other, col).wait_send()

    @pl.when(row == 0)
    def _():
        for n, d in enumerate(line_away):
            remote(strip, top.at[mine], top_send.at[n], topz_recv, at_row(*d), col).wait_send()

    for v in range(9):
        for g in range(2):
            if v + 9 * g < NC:
                to_col = v + 9 * g
                src = panel.at[:, pl.ds(PANEL * (v + 1 - g), PANEL)]

                @pl.when((row == g) & (col != to_col))
                def _():
                    remote(src, rows_ps.at[mine], ps_send.at[v], ps_recv.at[col], row, to_col).wait_send()

    for d in away:
        source = at_col(*d)
        where = pl.ds(pl.multiple_of(source * STRIP, STRIP), STRIP)
        landed(top.at[where], top_recv.at[source])
        landed(scale.at[source], s_recv.at[source])
        if d[1] != 0:
            landed(code.at[where, halves[0]], g_recv.at[0, source])
        if d[0] != 0:
            landed(code.at[where, halves[1]], g_recv.at[1, source])
    landed(scale.at[col], s_recv.at[col])
    for s in range(NS):
        for dz, dk in line:
            k, from_z = (core + dk) % 2, (z + dz) % 4
            landed(arrived.at[k, from_z, s], c2_recv.at[s, from_z, k])
    for copy in sends:
        copy.wait_send()


def exchange(slots, panel, child_one, child_two):
    vmem = pl.BlockSpec(memory_space=pltpu.VMEM)
    anywhere = pl.BlockSpec(memory_space=pl.ANY)
    dma = pltpu.SemaphoreType.DMA
    return pl.pallas_call(
        exchange_kernel,
        out_shape=(
            jax.ShapeDtypeStruct((PANEL, PANEL), F32),
            jax.ShapeDtypeStruct((PANEL, WIDTH), F32),
            jax.ShapeDtypeStruct((PANEL, ROWS), jnp.int16),
            jax.ShapeDtypeStruct((NC, ROWS // 128, 128), F32),
            jax.ShapeDtypeStruct((2, 4, NS, CAP, SUB, 128), BF16),
        ),
        in_specs=[pl.BlockSpec(memory_space=pltpu.SMEM), vmem, vmem, vmem],
        out_specs=(vmem, vmem, anywhere, anywhere, anywhere),
        scratch_shapes=[
            pltpu.VMEM((NS, 2, NC, SUB, 128), BF16),
            pltpu.VMEM((NS, NC, 2, SUB, 128), BF16),
            pltpu.VMEM((NS, 2 * NC, SUB, 128), BF16),
            pltpu.VMEM((NS, NR, CAP, SUB, 128), BF16),
            pltpu.VMEM((STRIP, ROWS), jnp.int16),
            pltpu.VMEM((ROWS // 128, 128), F32),
            dma((22,)), dma((NC,)), dma(()),
            dma((NS, NC, 2)), dma((NS, NC, 2)),
            dma((NS, NR)), dma((NS, 4, 2)),
            dma((2, 15)), dma((2, NC)),
            dma((15,)), dma((NC,)),
            dma((9,)), dma((NC,)),
            dma((4,)), dma(()),
        ],
        compiler_params=pltpu.CompilerParams(
            collective_id=0, has_side_effects=True, vmem_limit_bytes=48 * 1024 * 1024
        ),
    )(slots, panel, child_one, child_two)


def eliminate(block):
    lane = lax.broadcasted_iota(jnp.int32, (8, 128), 1)
    sub = lax.broadcasted_iota(jnp.int32, (8, 128), 0)
    v = [block[8 * h:8 * h + 8, :] for h in range(16)]
    for j in range(128):
        g, jj = j // 8, j % 8
        here = lane == j
        column = jnp.broadcast_to(v[g][:, j:j + 1], (8, 128))
        pivot = jnp.broadcast_to(column[jj:jj + 1, :], (8, 128))
        line = jnp.broadcast_to(v[g][jj:jj + 1, :], (8, 128))
        root = lax.rsqrt(pivot)
        inverse = root * root
        scaled = jnp.where(here, 1.0, line) * inverse
        below = sub > jj
        for h in range(g + 1, 16):
            factor = jnp.broadcast_to(v[h][:, j:j + 1], (8, 128))
            v[h] = jnp.where(here, 0.0, v[h]) - factor * scaled
        v[g] = jnp.where(
            below,
            jnp.where(here, 0.0, v[g]) - column * scaled,
            jnp.where(sub == jj, jnp.where(here, 1.0, v[g]) * root, v[g]),
        )
    return [jnp.where(lane <= 8 * h + sub, v[h], 0.0) for h in range(16)]


def solve_kernel(top, rows_ps, w_high, w_low, own_high, own_low, work, inverse):
    work[...] = top[...]
    blk = lax.broadcasted_iota(jnp.int32, (PANEL, PANEL), 1) // 128
    eye = (
        lax.broadcasted_iota(jnp.int32, (128, PANEL), 0)
        == lax.broadcasted_iota(jnp.int32, (128, PANEL), 1) % 128
    ).astype(F32)
    for k in range(4):
        rows = slice(128 * k, 128 * k + 128)
        for h, part in enumerate(eliminate(work[rows, rows])):
            inverse[8 * h:8 * h + 8, :] = part
        line = jnp.where(blk[:128] == k, eye, work[rows, :])
        done = jnp.dot(inverse[...], line, precision=HIGHEST, preferred_element_type=F32)
        work[rows, :] = done
        if k < 3:
            rest = slice(128 * k + 128, PANEL)
            count = PANEL - 128 * k - 128
            work[rest, :] = jnp.where(blk[:count] == k, 0.0, work[rest, :]) - lax.dot_general(
                done[:, rest], done, (((0,), (0,)), ((), ())),
                precision=HIGHEST, preferred_element_type=F32,
            )
    lower = lax.broadcasted_iota(jnp.int32, (PANEL, PANEL), 0) >= lax.broadcasted_iota(jnp.int32, (PANEL, PANEL), 1)
    work[...] = jnp.where(lower, work[...], 0.0)
    half = jnp.dot(work[...], rows_ps[...], precision=HIGHEST, preferred_element_type=F32)
    w = lax.dot_general(
        work[...], half, (((0,), (0,)), ((), ())), precision=HIGHEST, preferred_element_type=F32
    )
    high = w.astype(BF16)
    w_high[...] = high
    w_low[...] = (w - high.astype(F32)).astype(BF16)
    col = lax.axis_index("col")
    own = work[pl.ds(pl.multiple_of(col * STRIP, STRIP), STRIP), :]
    high = own.astype(BF16)
    own_high[...] = high
    own_low[...] = (own - high.astype(F32)).astype(BF16)


def solve(top, rows_ps):
    vmem = pl.BlockSpec(memory_space=pltpu.VMEM)
    return pl.pallas_call(
        solve_kernel,
        out_shape=(
            jax.ShapeDtypeStruct((PANEL, WIDTH), BF16),
            jax.ShapeDtypeStruct((PANEL, WIDTH), BF16),
            jax.ShapeDtypeStruct((STRIP, PANEL), BF16),
            jax.ShapeDtypeStruct((STRIP, PANEL), BF16),
        ),
        in_specs=[vmem, vmem],
        out_specs=(vmem,) * 4,
        scratch_shapes=[pltpu.VMEM((PANEL, PANEL), F32), pltpu.VMEM((128, 128), F32)],
        compiler_params=pltpu.CompilerParams(vmem_limit_bytes=40 * 1024 * 1024),
    )(top, rows_ps)


def update_kernel(
    where, has, slab, code, scale, first, second, w_high, w_low, own_high, own_low,
    out, factor, high_ref, low_ref,
):
    i = pl.program_id(0)
    row = lax.axis_index("row")
    for c in range(NC):
        part = slice(STRIP * c, STRIP * c + STRIP)
        for half in range(2):
            lanes = slice(128 * half, 128 * half + 128)
            step = scale[c, pl.ds(2 * i + half, 1), :]
            v = code[part, lanes].astype(jnp.int32).astype(F32) * step
            high = v.astype(BF16)
            high_ref[part, lanes] = high
            low_ref[part, lanes] = (v - high.astype(F32)).astype(BF16)
    high, low = high_ref[...], low_ref[...]

    def left(a, b):
        return lax.dot_general(a, b, (((0,), (0,)), ((), ())), preferred_element_type=F32)

    def right(a, b):
        return jnp.dot(a, b, preferred_element_type=F32)

    factor[...] = (
        right(own_high[...], high) + right(own_high[...], low) + right(own_low[...], high)
    )
    update = left(high, w_high[...]) + left(low, w_high[...]) + left(high, w_low[...])
    keep = (row * (ROWS // BLK) + i) >= PANEL // BLK
    update = jnp.where(keep, update, 0.0)
    for s in range(NS):
        rows = slice(SUB * s, SUB * s + SUB)
        for a in range(4):
            lanes = slice(128 * a, 128 * a + 128)
            one = jnp.where(has[i] > 0, first[0, a, s, 0].astype(F32), 0.0)
            two = jnp.where(has[ROWS // BLK + i] > 0, second[0, a, s, 0].astype(F32), 0.0)
            out[rows, lanes] = ((slab[rows, lanes] + one) + two) - update[rows, lanes]


def update(where, has, slab, code, scale, arrived, w_high, w_low, own_high, own_low):
    steps = ROWS // BLK

    def whole(shape):
        return pl.BlockSpec(shape, lambda i, w, h: (0,) * len(shape))

    def child(t):
        return pl.BlockSpec(
            (1, 4, NS, 1, SUB, 128), lambda i, w, h: (t, 0, 0, w[t * steps + i], 0, 0)
        )

    return pl.pallas_call(
        update_kernel,
        grid_spec=pltpu.PrefetchScalarGridSpec(
            num_scalar_prefetch=2,
            grid=(steps,),
            in_specs=[
                pl.BlockSpec((BLK, WIDTH), lambda i, w, h: (i, 0)),
                pl.BlockSpec((PANEL, BLK), lambda i, w, h: (0, i)),
                whole((NC, ROWS // 128, 128)),
                child(0),
                child(1),
                whole((PANEL, WIDTH)),
                whole((PANEL, WIDTH)),
                whole((STRIP, PANEL)),
                whole((STRIP, PANEL)),
            ],
            out_specs=[
                pl.BlockSpec((BLK, WIDTH), lambda i, w, h: (i, 0)),
                pl.BlockSpec((STRIP, BLK), lambda i, w, h: (0, i)),
            ],
            scratch_shapes=[pltpu.VMEM((PANEL, BLK), BF16), pltpu.VMEM((PANEL, BLK), BF16)],
        ),
        out_shape=(
            jax.ShapeDtypeStruct((ROWS, WIDTH), F32),
            jax.ShapeDtypeStruct((STRIP, ROWS), F32),
        ),
        compiler_params=pltpu.CompilerParams(vmem_limit_bytes=40 * 1024 * 1024),
    )(where, has, slab, code, scale, arrived, arrived, w_high, w_low, own_high, own_low)


def routing(maps):
    steps = ROWS // BLK
    owner = maps // steps
    count = maps.shape[1]
    before = jnp.arange(count)[None, :] < jnp.arange(count)[:, None]
    same = owner[:, :, None] == owner[:, None, :]
    rank = jnp.sum((same & before[None]).astype(jnp.int32), 2)
    slot = owner * CAP + rank
    hit = slot[:, None, :] == jnp.arange(NR * CAP)[None, :, None]
    slots = jnp.sum(jnp.where(hit, jnp.arange(count)[None, None, :], 0), 2)
    mine = lax.axis_index("row") * steps + jnp.arange(steps)
    at = maps[:, None, :] == mine[None, :, None]
    where = jnp.sum(jnp.where(at, rank[:, None, :], 0), 2)
    has = jnp.sum(at.astype(jnp.int32), 2)
    return tuple(v.reshape(-1).astype(jnp.int32) for v in (slots, where, has))


def per_device(front_panel, front_slab, child_one, child_two, map_one, map_two):
    slots, where, has = routing(jnp.stack([map_one, map_two]))
    top, rows_ps, code, scale, arrived = exchange(slots, front_panel.T, child_one, child_two)
    parts = solve(top, rows_ps)
    slab, factor = update(where, has, front_slab, code, scale, arrived, *parts)
    return (factor.T, slab)


def solution(mesh):
    in_specs = (P("row", "col"), P("row", "col"), P("col", "row"), P("col", "row"), P(), P())
    out_specs = (P("row", "col"), P("row", "col"))
    return jax.shard_map(
        per_device, mesh=mesh, in_specs=in_specs, out_specs=out_specs, check_vma=False
    )
```

```python
import functools

import jax
import jax.numpy as jnp
from jax import lax
from jax.experimental import pallas as pl
from jax.experimental.pallas import tpu as pltpu
from jax.sharding import PartitionSpec as P

BLK = 256
PANEL = 512
NC = 16
NR = 8
STRIP = 32
ROWS = 5120
HALF = ROWS // 2
WIDTH = 512
CAP = 8
NS = 2
SUB = BLK // NS
MESH = pl.DeviceIdType.MESH
F32 = jnp.float32
BF16 = jnp.bfloat16
HIGHEST = lax.Precision.HIGHEST


def swap_halves(v):
    return jnp.concatenate([v[:, 64:], v[:, :64]], axis=1)


def eliminate(block):
    lane = lax.broadcasted_iota(jnp.int32, (8, 128), 1)
    sub = lax.broadcasted_iota(jnp.int32, (8, 128), 0)
    v = [block[8 * h:8 * h + 8, :] for h in range(16)]

    def spread(h, j):
        return jnp.broadcast_to(v[h][:, j:j + 1], (8, 128))

    def line(tile, r):
        return jnp.broadcast_to(tile[r:r + 1, :], (8, 128))

    for g in range(16):
        base = 8 * g
        inside = (lane >= base) & (lane < base + 8)
        columns = [spread(g, base + i) for i in range(8)]
        a = {(r, i): line(columns[i], r) for i in range(8) for r in range(i, 8)}
        lines = [jnp.where(inside, (lane == base + r).astype(F32), line(v[g], r)) for r in range(8)]
        rest = {h: [spread(h, base + i) for i in range(8)] for h in range(g + 1, 16)}
        for h in range(g + 1, 16):
            v[h] = jnp.where(inside, 0.0, v[h])
        for j in range(8):
            root = lax.rsqrt(a[j, j])
            for i in range(j + 1, 8):
                a[i, j] = a[i, j] * root
            for k in range(j + 1, 8):
                for i in range(k, 8):
                    a[i, k] = a[i, k] - a[i, j] * a[k, j]
            lines[j] = lines[j] * root
            for r in range(j + 1, 8):
                lines[r] = lines[r] - a[r, j] * lines[j]
            for h in range(g + 1, 16):
                f = rest[h][j] * root
                for i in range(j + 1, 8):
                    rest[h][i] = rest[h][i] - a[i, j] * f
                v[h] = v[h] - f * lines[j]
        out = lines[0]
        for r in range(1, 8):
            out = jnp.where(sub == r, lines[r], out)
        v[g] = out
    return [jnp.where(lane <= 8 * h + sub, v[h], 0.0) for h in range(16)]


def halve(v):
    high = v.astype(BF16)
    return high, (v - high.astype(F32)).astype(BF16)


def exchange_kernel(
    slots, panel, child_one, child_two, slab_hbm,
    code, scale, arrived, slab, w_high, w_low, own_high, own_low,
    pack, got, blocks, outgoing, coded, scales, ps_scales,
    top, ps_code, ps_scale, work, inverse, rows_ps,
    load, top_send, topz_recv, top_recv, topx_recv, c1_send, c1_recv, c2_send, c2_recv,
    g_send, g_recv, g3_recv, s_send, s_recv, ps_send, ps_recv, psb_send, psb_recv,
):
    row = lax.axis_index("row")
    col = lax.axis_index("col")
    z, core = row // 2, row % 2
    x, y = col // 4, col % 4
    other = z * 2 + (1 - core)

    def at_col(dx, dy):
        return ((x + dx) % 4) * 4 + (y + dy) % 4

    def at_row(dz, dk):
        return ((z + dz) % 4) * 2 + (core + dk) % 2

    def strip_of(source):
        return pl.ds(pl.multiple_of(source * STRIP, STRIP), STRIP)

    plane = [(dx, dy) for dx in range(4) for dy in range(4)]
    away = [d for d in plane if d != (0, 0)]
    line = [(dz, dk) for dz in range(4) for dk in range(2)]
    line_away = [d for d in line if d != (0, 0)]
    mine = strip_of(col)

    slab_load = pltpu.make_async_copy(slab_hbm, slab, load)

    barrier = pltpu.get_barrier_semaphore()
    for d in away:
        pl.semaphore_signal(barrier, inc=1, device_id=(row, at_col(*d)), device_id_type=MESH)
    for d in plane:
        pl.semaphore_signal(barrier, inc=1, device_id=(other, at_col(*d)), device_id_type=MESH)
    for dz in range(1, 4):
        for dk in range(2):
            pl.semaphore_signal(barrier, inc=1, device_id=(at_row(dz, dk), col), device_id_type=MESH)
    pl.semaphore_wait(barrier, 37)

    sends = []

    def remote(src, dst, send, recv, to_row, to_col):
        return pltpu.make_async_remote_copy(
            src_ref=src, dst_ref=dst, send_sem=send, recv_sem=recv,
            device_id=(to_row, to_col), device_id_type=MESH,
        )

    def push(*args):
        copy = remote(*args)
        copy.start()
        sends.append(copy)

    def landed(ref, sem):
        pltpu.make_async_copy(ref, ref, sem).wait()

    def top_half(k):
        return pl.ds(pl.multiple_of(k * 256, 256), 256)

    def top_out(n, d):
        lanes = pl.ds(256 * d[1], 256)
        return remote(panel.at[:, lanes], top.at[mine, lanes], top_send.at[n], topz_recv, at_row(*d), col)

    @pl.when(row == 0)
    def _():
        for n, d in enumerate(line_away):
            top_out(n, d).start()
        pltpu.make_async_copy(panel.at[:, pl.ds(0, 256)], top.at[mine, pl.ds(0, 256)], topz_recv).start()

    low = lax.broadcasted_iota(jnp.int32, (SUB, 128), 1) < 64

    def columns_hop(s):
        for t, child in enumerate((child_one, child_two)):
            for p in range(NC // 2):
                lanes = slice(128 * p, 128 * p + 128)
                first = child[s * SUB:(s + 1) * SUB, lanes]
                second = child[BLK + s * SUB:BLK + (s + 1) * SUB, lanes]
                pack[s, t, 2 * p] = jnp.where(low, first, swap_halves(second))
                pack[s, t, 2 * p + 1] = jnp.where(low, swap_halves(first), second)
        for n, d in enumerate(plane):
            for dk in range(2):
                to = (core + dk) % 2
                src = pack.at[s, to, at_col(*d)]
                dst = got.at[s, col, core]
                if d == (0, 0) and dk == 0:
                    pltpu.make_async_copy(src, dst, c1_recv.at[s, col, core]).start()
                else:
                    push(src, dst, c1_send.at[s, n, dk], c1_recv.at[s, col, core], z * 2 + to, at_col(*d))

    def rows_hop(s):
        for d in plane:
            for dk in range(2):
                source, k = at_col(*d), (core + dk) % 2
                landed(got.at[s, source, k], c1_recv.at[s, source, k])
        for c in range(NC):
            first = got[s, c, 0]
            second = got[s, c, 1]
            blocks[s, 2 * c] = jnp.where(low, first, swap_halves(second))
            blocks[s, 2 * c + 1] = jnp.where(low, swap_halves(first), second)
        for n, d in enumerate(line):
            to = at_row(*d)
            for q in range(CAP):
                outgoing[s, to, q] = blocks[s, slots[core * NR * CAP + to * CAP + q]]
            dst = arrived.at[core, z, s]
            if d == (0, 0):
                pltpu.make_async_copy(outgoing.at[s, to], dst, c2_recv.at[s, z, core]).start()
            else:
                push(outgoing.at[s, to], dst, c2_send.at[s, n], c2_recv.at[s, z, core], to, col)

    def top_hop():
        lanes = top_half(core)
        landed(top.at[mine, lanes], topz_recv)
        for n, d in enumerate(away):
            push(top.at[mine, lanes], top.at[mine, lanes], top_send.at[7 + n], top_recv.at[col], row, at_col(*d))

    def top_swap():
        lanes = top_half(core)
        for d in away:
            source = at_col(*d)
            landed(top.at[strip_of(source), lanes], top_recv.at[source])
        push(top.at[:, lanes], top.at[:, lanes], top_send.at[22], topx_recv, other, col)

    def code_panel():
        for j in range(ROWS // 128):
            lanes = slice(128 * j, 128 * j + 128)
            v = panel[:, lanes]
            most = jnp.maximum(jnp.max(jnp.abs(v), axis=0, keepdims=True), 1e-30)
            step = most * (1.0 / 32760.0)
            coded[:, lanes] = jnp.round(v * (1.0 / step)).astype(jnp.int32).astype(jnp.int16)
            scales[j:j + 1, :] = step
            ps_scales[j // 4, j % 4:j % 4 + 1, :] = step
            ps_scales[j // 4, j % 4 + 4:j % 4 + 5, :] = step

    def ps_out(v, g):
        to_col = v + 9 * g
        unit = v + 1 - g
        part = coded.at[:, pl.ds(PANEL * unit, PANEL)]
        return (
            (part, ps_code.at[mine], ps_send.at[0, v], ps_recv.at[0, col], row, to_col),
            (ps_scales.at[unit], ps_scale.at[col], ps_send.at[1, v], ps_recv.at[1, col], row, to_col),
        )

    ps_pairs = [(v, g) for v in range(9) for g in range(2) if v + 9 * g < NC]

    def ps_first():
        for v, g in ps_pairs:
            @pl.when((row == g) & (col != v + 9 * g))
            def _():
                for args in ps_out(v, g):
                    remote(*args).start()

            @pl.when((row == g) & (col == v + 9 * g))
            def _():
                for args in ps_out(v, g):
                    pltpu.make_async_copy(args[0], args[1], args[3]).start()

    root = jnp.where(col < 9, 0, 1)

    def ps_copies(n, d):
        return (
            remote(ps_code, ps_code, psb_send.at[0, n], psb_recv.at[0], at_row(*d), col),
            remote(ps_scale, ps_scale, psb_send.at[1, n], psb_recv.at[1], at_row(*d), col),
        )

    from_root = list(enumerate(((1, 0), (3, 0), (2, 0), (0, 1))))

    def ps_second():
        @pl.when(row == root)
        def _():
            for d in plane:
                source = at_col(*d)
                landed(ps_code.at[strip_of(source)], ps_recv.at[0, source])
                landed(ps_scale.at[source], ps_recv.at[1, source])
            for n, d in from_root:
                for copy in ps_copies(n, d):
                    copy.start()

    def ps_third():
        @pl.when(row != root)
        def _():
            landed(ps_code, psb_recv.at[0])
            landed(ps_scale, psb_recv.at[1])

        @pl.when((core == root) & (z > 0))
        def _():
            for copy in ps_copies(3, (0, 1)):
                copy.start()

    halves = [pl.ds(0, HALF), pl.ds(HALF, HALF)]

    def along(h, n, m):
        return at_col(n, m) if h == 0 else at_col(m, n)

    def gather_first():
        pltpu.make_async_copy(scales, scale.at[col], s_recv.at[col]).start()
        for h in range(2):
            part = coded.at[:, halves[h]]
            pltpu.make_async_copy(part, code.at[mine, halves[h]], g_recv.at[h, col]).start()
            for n in (1, 3, 2):
                push(part, code.at[mine, halves[h]], g_send.at[h, n - 1], g_recv.at[h, col], row, along(h, n, 0))
        for n, d in enumerate(away):
            push(scales, scale.at[col], s_send.at[n], s_recv.at[col], row, at_col(*d))

    def gather_second():
        for n in range(4):
            for h in range(2):
                source = along(h, n, 0)
                part = code.at[strip_of(source), halves[h]]
                landed(part, g_recv.at[h, source])
                for m in (1, 3):
                    push(part, part, g_send.at[h, 3 + 2 * n + m // 2], g_recv.at[h, source], row, along(h, 0, m))

    def quarter(h, q):
        return pl.ds(HALF * h + HALF // 2 * q, HALF // 2)

    def gather_third():
        for n in range(4):
            for h in range(2):
                for q, m in enumerate((3, 1)):
                    source = along(h, n, m)
                    landed(code.at[strip_of(source), halves[h]], g_recv.at[h, source])
                    part = code.at[strip_of(source), quarter(h, q)]
                    to = along(h, 0, 1 if q == 0 else 3)
                    push(part, part, g_send.at[h, 11 + 2 * n + q], g3_recv.at[h, n, q], row, to)

    blk = lax.broadcasted_iota(jnp.int32, (PANEL, PANEL), 1) // 128
    eye = (
        lax.broadcasted_iota(jnp.int32, (128, PANEL), 0)
        == lax.broadcasted_iota(jnp.int32, (128, PANEL), 1) % 128
    ).astype(F32)

    def factor_start():
        landed(top.at[:, top_half(1 - core)], topx_recv)
        work[...] = top[...]

    def factor_step(k):
        rows = slice(128 * k, 128 * k + 128)
        for h, part in enumerate(eliminate(work[rows, rows])):
            inverse[8 * h:8 * h + 8, :] = part
        entry = jnp.where(blk[:128] == k, eye, work[rows, :])
        done = jnp.dot(inverse[...], entry, precision=HIGHEST, preferred_element_type=F32)
        work[rows, :] = done
        if k < 3:
            rest = slice(128 * k + 128, PANEL)
            count = PANEL - 128 * k - 128
            work[rest, :] = jnp.where(blk[:count] == k, 0.0, work[rest, :]) - lax.dot_general(
                done[:, rest], done, (((0,), (0,)), ((), ())),
                precision=HIGHEST, preferred_element_type=F32,
            )

    def factor_end():
        lower = lax.broadcasted_iota(jnp.int32, (PANEL, PANEL), 0) >= lax.broadcasted_iota(
            jnp.int32, (PANEL, PANEL), 1
        )
        work[...] = jnp.where(lower, work[...], 0.0)
        own_high[...], own_low[...] = halve(work[mine, :])

    def weights():
        for c in range(NC):
            part = slice(STRIP * c, STRIP * c + STRIP)
            for j in range(4):
                lanes = slice(128 * j, 128 * j + 128)
                rows_ps[part, lanes] = ps_code[part, lanes].astype(jnp.int32).astype(F32) * ps_scale[c, j:j + 1, :]
        half = jnp.dot(work[...], rows_ps[...], precision=HIGHEST, preferred_element_type=F32)
        w_high[...], w_low[...] = halve(
            lax.dot_general(
                work[...], half, (((0,), (0,)), ((), ())), precision=HIGHEST, preferred_element_type=F32
            )
        )

    columns_hop(0)
    slab_load.start()
    top_hop()
    columns_hop(1)
    code_panel()
    gather_first()
    ps_first()
    top_swap()
    rows_hop(0)
    factor_start()
    factor_step(0)
    gather_second()
    factor_step(1)
    rows_hop(1)
    ps_second()
    factor_step(2)
    gather_third()
    factor_step(3)
    ps_third()
    factor_end()
    weights()

    landed(scale.at[col], s_recv.at[col])
    for d in away:
        landed(scale.at[at_col(*d)], s_recv.at[at_col(*d)])
    for h in range(2):
        for n in range(4):
            source = along(h, n, 2)
            for q in range(2):
                landed(code.at[strip_of(source), quarter(h, q)], g3_recv.at[h, n, q])
    for s in range(NS):
        for dz, dk in line:
            k, from_z = (core + dk) % 2, (z + dz) % 4
            landed(arrived.at[k, from_z, s], c2_recv.at[s, from_z, k])
    slab_load.wait()
    for copy in sends:
        copy.wait_send()

    @pl.when(row == 0)
    def _():
        for n, d in enumerate(line_away):
            top_out(n, d).wait_send()

    for v, g in ps_pairs:
        @pl.when((row == g) & (col != v + 9 * g))
        def _():
            for args in ps_out(v, g):
                remote(*args).wait_send()

    @pl.when(row == root)
    def _():
        for n, d in from_root:
            for copy in ps_copies(n, d):
                copy.wait_send()

    @pl.when((core == root) & (z > 0))
    def _():
        for copy in ps_copies(3, (0, 1)):
            copy.wait_send()


def exchange(slots, panel, child_one, child_two, slab):
    vmem = pl.BlockSpec(memory_space=pltpu.VMEM)
    hbm = pl.BlockSpec(memory_space=pltpu.HBM)
    dma = pltpu.SemaphoreType.DMA
    return pl.pallas_call(
        exchange_kernel,
        out_shape=(
            jax.ShapeDtypeStruct((PANEL, ROWS), jnp.int16),
            jax.ShapeDtypeStruct((NC, ROWS // 128, 128), F32),
            jax.ShapeDtypeStruct((2, 4, NS, CAP, SUB, 128), BF16),
            jax.ShapeDtypeStruct((ROWS, WIDTH), F32),
            jax.ShapeDtypeStruct((PANEL, WIDTH), BF16),
            jax.ShapeDtypeStruct((PANEL, WIDTH), BF16),
            jax.ShapeDtypeStruct((STRIP, PANEL), BF16),
            jax.ShapeDtypeStruct((STRIP, PANEL), BF16),
        ),
        in_specs=[pl.BlockSpec(memory_space=pltpu.SMEM)] + [vmem] * 3 + [hbm],
        out_specs=(vmem,) * 8,
        scratch_shapes=[
            pltpu.VMEM((NS, 2, NC, SUB, 128), BF16),
            pltpu.VMEM((NS, NC, 2, SUB, 128), BF16),
            pltpu.VMEM((NS, 2 * NC, SUB, 128), BF16),
            pltpu.VMEM((NS, NR, CAP, SUB, 128), BF16),
            pltpu.VMEM((STRIP, ROWS), jnp.int16),
            pltpu.VMEM((ROWS // 128, 128), F32),
            pltpu.VMEM((ROWS // PANEL, 8, 128), F32),
            pltpu.VMEM((PANEL, PANEL), F32),
            pltpu.VMEM((PANEL, WIDTH), jnp.int16),
            pltpu.VMEM((NC, 8, 128), F32),
            pltpu.VMEM((PANEL, PANEL), F32),
            pltpu.VMEM((128, 128), F32),
            pltpu.VMEM((PANEL, WIDTH), F32),
            dma(()),
            dma((23,)), dma(()), dma((NC,)), dma(()),
            dma((NS, NC, 2)), dma((NS, NC, 2)),
            dma((NS, NR)), dma((NS, 4, 2)),
            dma((2, 19)), dma((2, NC)), dma((2, 4, 2)),
            dma((15,)), dma((NC,)),
            dma((2, 9)), dma((2, NC)),
            dma((2, 4)), dma((2,)),
        ],
        compiler_params=pltpu.CompilerParams(
            collective_id=0, has_side_effects=True, vmem_limit_bytes=26 * 1024 * 1024
        ),
    )(slots, panel, child_one, child_two, slab)


STEP = 512


def update_kernel(
    where, has, slab, code, scale, arrived, w_high, w_low, own_high, own_low, out, factor, rows_t,
):
    i = pl.program_id(0)
    row = lax.axis_index("row")
    tiles = STEP // 128
    for j in range(tiles):
        lanes = pl.ds(pl.multiple_of(i * STEP + 128 * j, 128), 128)
        for c in range(NC):
            part = slice(STRIP * c, STRIP * c + STRIP)
            rows_t[part, 128 * j:128 * j + 128] = (
                code[part, lanes].astype(jnp.int32).astype(F32) * scale[c, pl.ds(tiles * i + j, 1), :]
            )
    high, low = halve(rows_t[...])

    def dot(a, b):
        return jnp.dot(a, b, preferred_element_type=F32)

    factor[...] = dot(own_high[...], high) + dot(own_high[...], low) + dot(own_low[...], high)
    high, low = high.T, low.T
    update = dot(high, w_high[...]) + dot(low, w_high[...]) + dot(high, w_low[...])
    keep = (row * (ROWS // STEP) + i) >= PANEL // STEP
    update = jnp.where(keep, update, 0.0)
    for n in range(STEP // BLK):
        block = i * (STEP // BLK) + n
        one_at, two_at = where[block], where[ROWS // BLK + block]
        one_in, two_in = has[block] > 0, has[ROWS // BLK + block] > 0
        for s in range(NS):
            rows = slice(BLK * n + SUB * s, BLK * n + SUB * s + SUB)
            here = pl.ds(pl.multiple_of(i * STEP + BLK * n + SUB * s, SUB), SUB)
            for a in range(4):
                lanes = slice(128 * a, 128 * a + 128)
                one = jnp.where(one_in, arrived[0, a, s, one_at].astype(F32), 0.0)
                two = jnp.where(two_in, arrived[1, a, s, two_at].astype(F32), 0.0)
                out[rows, lanes] = ((slab[here, lanes] + one) + two) - update[rows, lanes]


def update(where, has, slab, code, scale, arrived, w_high, w_low, own_high, own_low):
    vmem = pl.BlockSpec(memory_space=pltpu.VMEM)
    return pl.pallas_call(
        update_kernel,
        grid_spec=pltpu.PrefetchScalarGridSpec(
            num_scalar_prefetch=2,
            grid=(ROWS // STEP,),
            in_specs=[vmem] * 8,
            out_specs=[
                pl.BlockSpec((STEP, WIDTH), lambda i, w, h: (i, 0)),
                pl.BlockSpec((STRIP, STEP), lambda i, w, h: (0, i)),
            ],
            scratch_shapes=[pltpu.VMEM((PANEL, STEP), F32)],
        ),
        out_shape=(
            jax.ShapeDtypeStruct((ROWS, WIDTH), F32),
            jax.ShapeDtypeStruct((STRIP, ROWS), F32),
        ),
        compiler_params=pltpu.CompilerParams(vmem_limit_bytes=16 * 1024 * 1024),
    )(where, has, slab, code, scale, arrived, w_high, w_low, own_high, own_low)


def routing(maps):
    steps = ROWS // BLK
    owner = maps // steps
    count = maps.shape[1]
    before = jnp.arange(count)[None, :] < jnp.arange(count)[:, None]
    same = owner[:, :, None] == owner[:, None, :]
    rank = jnp.sum((same & before[None]).astype(jnp.int32), 2)
    slot = owner * CAP + rank
    hit = slot[:, None, :] == jnp.arange(NR * CAP)[None, :, None]
    slots = jnp.sum(jnp.where(hit, jnp.arange(count)[None, None, :], 0), 2)
    mine = lax.axis_index("row") * steps + jnp.arange(steps)
    at = maps[:, None, :] == mine[None, :, None]
    where = jnp.sum(jnp.where(at, rank[:, None, :], 0), 2)
    has = jnp.sum(at.astype(jnp.int32), 2)
    return tuple(v.reshape(-1).astype(jnp.int32) for v in (slots, where, has))


def per_device(front_panel, front_slab, child_one, child_two, map_one, map_two):
    slots, where, has = routing(jnp.stack([map_one, map_two]))
    code, scale, arrived, slab, *parts = exchange(slots, front_panel.T, child_one, child_two, front_slab)
    slab, factor = update(where, has, slab, code, scale, arrived, *parts)
    return (factor.T, slab)


def solution(mesh):
    in_specs = (P("row", "col"), P("row", "col"), P("col", "row"), P("col", "row"), P(), P())
    out_specs = (P("row", "col"), P("row", "col"))
    return jax.shard_map(
        per_device, mesh=mesh, in_specs=in_specs, out_specs=out_specs, check_vma=False
    )
```

```python
import functools

import jax
import jax.numpy as jnp
from jax import lax
from jax.experimental import pallas as pl
from jax.experimental.pallas import tpu as pltpu
from jax.sharding import PartitionSpec as P

BLK = 256
PANEL = 512
NC = 16
NR = 8
STRIP = 32
ROWS = 5120
HALF = ROWS // 2
WIDTH = 512
CAP = 8
NS = 4
SUB = BLK // NS
STEP = 512
MESH = pl.DeviceIdType.MESH
F32 = jnp.float32
BF16 = jnp.bfloat16
HIGHEST = lax.Precision.HIGHEST


def swap_halves(v):
    return jnp.concatenate([v[:, 64:], v[:, :64]], axis=1)


def eliminate(block):
    lane = lax.broadcasted_iota(jnp.int32, (8, 128), 1)
    sub = lax.broadcasted_iota(jnp.int32, (8, 128), 0)
    v = [block[8 * h:8 * h + 8, :] for h in range(16)]

    def spread(h, j):
        return jnp.broadcast_to(v[h][:, j:j + 1], (8, 128))

    def line(tile, r):
        return jnp.broadcast_to(tile[r:r + 1, :], (8, 128))

    for g in range(16):
        base = 8 * g
        inside = (lane >= base) & (lane < base + 8)
        columns = [spread(g, base + i) for i in range(8)]
        a = {(r, i): line(columns[i], r) for i in range(8) for r in range(i, 8)}
        lines = [jnp.where(inside, (lane == base + r).astype(F32), line(v[g], r)) for r in range(8)]
        rest = {h: [spread(h, base + i) for i in range(8)] for h in range(g + 1, 16)}
        for h in range(g + 1, 16):
            v[h] = jnp.where(inside, 0.0, v[h])
        for j in range(8):
            root = lax.rsqrt(a[j, j])
            for i in range(j + 1, 8):
                a[i, j] = a[i, j] * root
            for k in range(j + 1, 8):
                for i in range(k, 8):
                    a[i, k] = a[i, k] - a[i, j] * a[k, j]
            lines[j] = lines[j] * root
            for r in range(j + 1, 8):
                lines[r] = lines[r] - a[r, j] * lines[j]
            for h in range(g + 1, 16):
                f = rest[h][j] * root
                for i in range(j + 1, 8):
                    rest[h][i] = rest[h][i] - a[i, j] * f
                v[h] = v[h] - f * lines[j]
        out = lines[0]
        for r in range(1, 8):
            out = jnp.where(sub == r, lines[r], out)
        v[g] = out
    return [jnp.where(lane <= 8 * h + sub, v[h], 0.0) for h in range(16)]


def halve(v):
    high = v.astype(BF16)
    return high, (v - high.astype(F32)).astype(BF16)


def exchange_kernel(
    slots, panel, child_one, child_two, slab_hbm,
    arrived, slab, factor,
    code, scale, w_high, w_low, own_high, own_low, rows_t, pack, got, blocks, outgoing, coded, scales, ps_scales,
    top, ps_code, ps_scale, work, inverse, rows_ps,
    load, top_send, topz_recv, top_recv, topx_recv, c1_send, c1_recv, c2_send, c2_recv,
    g_send, g_recv, g3_recv, s_send, s_recv, ps_send, ps_recv, psb_send, psb_recv,
):
    row = lax.axis_index("row")
    col = lax.axis_index("col")
    z, core = row // 2, row % 2
    x, y = col // 4, col % 4
    other = z * 2 + (1 - core)

    def at_col(dx, dy):
        return ((x + dx) % 4) * 4 + (y + dy) % 4

    def at_row(dz, dk):
        return ((z + dz) % 4) * 2 + (core + dk) % 2

    def strip_of(source):
        return pl.ds(pl.multiple_of(source * STRIP, STRIP), STRIP)

    plane = [(dx, dy) for dx in range(4) for dy in range(4)]
    away = [d for d in plane if d != (0, 0)]
    line = [(dz, dk) for dz in range(4) for dk in range(2)]
    line_away = [d for d in line if d != (0, 0)]
    mine = strip_of(col)

    slab_load = pltpu.make_async_copy(slab_hbm, slab, load)

    barrier = pltpu.get_barrier_semaphore()
    for d in away:
        pl.semaphore_signal(barrier, inc=1, device_id=(row, at_col(*d)), device_id_type=MESH)
    for d in plane:
        pl.semaphore_signal(barrier, inc=1, device_id=(other, at_col(*d)), device_id_type=MESH)
    for dz in range(1, 4):
        for dk in range(2):
            pl.semaphore_signal(barrier, inc=1, device_id=(at_row(dz, dk), col), device_id_type=MESH)
    sends = []

    def remote(src, dst, send, recv, to_row, to_col):
        return pltpu.make_async_remote_copy(
            src_ref=src, dst_ref=dst, send_sem=send, recv_sem=recv,
            device_id=(to_row, to_col), device_id_type=MESH,
        )

    def push(*args):
        copy = remote(*args)
        copy.start()
        sends.append(copy)

    def landed(ref, sem):
        pltpu.make_async_copy(ref, ref, sem).wait()

    def top_half(k):
        return pl.ds(pl.multiple_of(k * 256, 256), 256)

    def top_out(n, d):
        lanes = pl.ds(256 * d[1], 256)
        return remote(panel.at[:, lanes], top.at[mine, lanes], top_send.at[n], topz_recv, at_row(*d), col)

    def top_first():
        @pl.when(row == 0)
        def _():
            for n, d in enumerate(line_away):
                top_out(n, d).start()
            pltpu.make_async_copy(panel.at[:, pl.ds(0, 256)], top.at[mine, pl.ds(0, 256)], topz_recv).start()

    low = lax.broadcasted_iota(jnp.int32, (SUB, 128), 1) < 64

    def columns_pack(s):
        for t, child in enumerate((child_one, child_two)):
            for p in range(NC // 2):
                lanes = slice(128 * p, 128 * p + 128)
                first = child[s * SUB:(s + 1) * SUB, lanes]
                second = child[BLK + s * SUB:BLK + (s + 1) * SUB, lanes]
                pack[s, t, 2 * p] = jnp.where(low, first, swap_halves(second))
                pack[s, t, 2 * p + 1] = jnp.where(low, swap_halves(first), second)

    def columns_hop(s):
        for n, d in enumerate(plane):
            for dk in range(2):
                to = (core + dk) % 2
                src = pack.at[s, to, at_col(*d)]
                dst = got.at[s, col, core]
                if d == (0, 0) and dk == 0:
                    pltpu.make_async_copy(src, dst, c1_recv.at[s, col, core]).start()
                else:
                    push(src, dst, c1_send.at[s, n, dk], c1_recv.at[s, col, core], z * 2 + to, at_col(*d))

    def rows_hop(s):
        for d in plane:
            for dk in range(2):
                source, k = at_col(*d), (core + dk) % 2
                landed(got.at[s, source, k], c1_recv.at[s, source, k])
        for c in range(NC):
            first = got[s, c, 0]
            second = got[s, c, 1]
            blocks[s, 2 * c] = jnp.where(low, first, swap_halves(second))
            blocks[s, 2 * c + 1] = jnp.where(low, swap_halves(first), second)
        for n, d in enumerate(line):
            to = at_row(*d)
            for q in range(CAP):
                outgoing[s, to, q] = blocks[s, slots[core * NR * CAP + to * CAP + q]]
            dst = arrived.at[core, z, s]
            if d == (0, 0):
                pltpu.make_async_copy(outgoing.at[s, to], dst, c2_recv.at[s, z, core]).start()
            else:
                push(outgoing.at[s, to], dst, c2_send.at[s, n], c2_recv.at[s, z, core], to, col)

    def top_hop():
        lanes = top_half(core)
        landed(top.at[mine, lanes], topz_recv)
        for n, d in enumerate(away):
            push(top.at[mine, lanes], top.at[mine, lanes], top_send.at[7 + n], top_recv.at[col], row, at_col(*d))

    def top_swap():
        lanes = top_half(core)
        for d in away:
            source = at_col(*d)
            landed(top.at[strip_of(source), lanes], top_recv.at[source])
        push(top.at[:, lanes], top.at[:, lanes], top_send.at[22], topx_recv, other, col)

    def code_panel():
        for j in range(ROWS // 128):
            lanes = slice(128 * j, 128 * j + 128)
            v = panel[:, lanes]
            most = jnp.maximum(jnp.max(jnp.abs(v), axis=0, keepdims=True), 1e-30)
            step = most * (1.0 / 32760.0)
            coded[:, lanes] = jnp.round(v * (1.0 / step)).astype(jnp.int32).astype(jnp.int16)
            scales[j:j + 1, :] = step
            ps_scales[j // 4, j % 4:j % 4 + 1, :] = step
            ps_scales[j // 4, j % 4 + 4:j % 4 + 5, :] = step

    def ps_out(v, g):
        to_col = v + 9 * g
        unit = v + 1 - g
        part = coded.at[:, pl.ds(PANEL * unit, PANEL)]
        return (
            (part, ps_code.at[mine], ps_send.at[0, v], ps_recv.at[0, col], row, to_col),
            (ps_scales.at[unit], ps_scale.at[col], ps_send.at[1, v], ps_recv.at[1, col], row, to_col),
        )

    ps_pairs = [(v, g) for v in range(9) for g in range(2) if v + 9 * g < NC]

    def ps_first():
        for v, g in ps_pairs:
            @pl.when((row == g) & (col != v + 9 * g))
            def _():
                for args in ps_out(v, g):
                    remote(*args).start()

            @pl.when((row == g) & (col == v + 9 * g))
            def _():
                for args in ps_out(v, g):
                    pltpu.make_async_copy(args[0], args[1], args[3]).start()

    root = jnp.where(col < 9, 0, 1)

    def ps_copies(n, d):
        return (
            remote(ps_code, ps_code, psb_send.at[0, n], psb_recv.at[0], at_row(*d), col),
            remote(ps_scale, ps_scale, psb_send.at[1, n], psb_recv.at[1], at_row(*d), col),
        )

    from_root = list(enumerate(((1, 0), (3, 0), (2, 0), (0, 1))))

    def ps_second():
        @pl.when(row == root)
        def _():
            for d in plane:
                source = at_col(*d)
                landed(ps_code.at[strip_of(source)], ps_recv.at[0, source])
                landed(ps_scale.at[source], ps_recv.at[1, source])
            for n, d in from_root:
                for copy in ps_copies(n, d):
                    copy.start()

    def ps_third():
        @pl.when(row != root)
        def _():
            landed(ps_code, psb_recv.at[0])
            landed(ps_scale, psb_recv.at[1])

        @pl.when((core == root) & (z > 0))
        def _():
            for copy in ps_copies(3, (0, 1)):
                copy.start()

    halves = [pl.ds(0, HALF), pl.ds(HALF, HALF)]

    def along(h, n, m):
        return at_col(n, m) if h == 0 else at_col(m, n)

    def gather_first():
        pltpu.make_async_copy(scales, scale.at[col], s_recv.at[col]).start()
        for h in range(2):
            part = coded.at[:, halves[h]]
            pltpu.make_async_copy(part, code.at[mine, halves[h]], g_recv.at[h, col]).start()
            for n in (1, 3, 2):
                push(part, code.at[mine, halves[h]], g_send.at[h, n - 1], g_recv.at[h, col], row, along(h, n, 0))
        for n, d in enumerate(away):
            push(scales, scale.at[col], s_send.at[n], s_recv.at[col], row, at_col(*d))

    def gather_second():
        for n in range(4):
            for h in range(2):
                source = along(h, n, 0)
                part = code.at[strip_of(source), halves[h]]
                landed(part, g_recv.at[h, source])
                for m in (1, 3):
                    push(part, part, g_send.at[h, 3 + 2 * n + m // 2], g_recv.at[h, source], row, along(h, 0, m))

    def quarter(h, q):
        return pl.ds(HALF * h + HALF // 2 * q, HALF // 2)

    def gather_third():
        for n in range(4):
            for h in range(2):
                for q, m in enumerate((3, 1)):
                    source = along(h, n, m)
                    landed(code.at[strip_of(source), halves[h]], g_recv.at[h, source])
                    part = code.at[strip_of(source), quarter(h, q)]
                    to = along(h, 0, 1 if q == 0 else 3)
                    push(part, part, g_send.at[h, 11 + 2 * n + q], g3_recv.at[h, n, q], row, to)

    def gather_end():
        landed(scale.at[col], s_recv.at[col])
        for d in away:
            landed(scale.at[at_col(*d)], s_recv.at[at_col(*d)])
        for h in range(2):
            for n in range(4):
                source = along(h, n, 2)
                for q in range(2):
                    landed(code.at[strip_of(source), quarter(h, q)], g3_recv.at[h, n, q])

    blk = lax.broadcasted_iota(jnp.int32, (PANEL, PANEL), 1) // 128
    eye = (
        lax.broadcasted_iota(jnp.int32, (128, PANEL), 0)
        == lax.broadcasted_iota(jnp.int32, (128, PANEL), 1) % 128
    ).astype(F32)

    def factor_start():
        landed(top.at[:, top_half(1 - core)], topx_recv)
        work[...] = top[...]

    def factor_step(k):
        rows = slice(128 * k, 128 * k + 128)
        for h, part in enumerate(eliminate(work[rows, rows])):
            inverse[8 * h:8 * h + 8, :] = part
        entry = jnp.where(blk[:128] == k, eye, work[rows, :])
        done = jnp.dot(inverse[...], entry, precision=HIGHEST, preferred_element_type=F32)
        work[rows, :] = done
        if k < 3:
            rest = slice(128 * k + 128, PANEL)
            count = PANEL - 128 * k - 128
            work[rest, :] = jnp.where(blk[:count] == k, 0.0, work[rest, :]) - lax.dot_general(
                done[:, rest], done, (((0,), (0,)), ((), ())),
                precision=HIGHEST, preferred_element_type=F32,
            )

    def factor_end():
        lower = lax.broadcasted_iota(jnp.int32, (PANEL, PANEL), 0) >= lax.broadcasted_iota(
            jnp.int32, (PANEL, PANEL), 1
        )
        work[...] = jnp.where(lower, work[...], 0.0)
        own_high[...], own_low[...] = halve(work[mine, :])

    def weights():
        for c in range(NC):
            part = slice(STRIP * c, STRIP * c + STRIP)
            for j in range(4):
                lanes = slice(128 * j, 128 * j + 128)
                rows_ps[part, lanes] = ps_code[part, lanes].astype(jnp.int32).astype(F32) * ps_scale[c, j:j + 1, :]
        half = jnp.dot(work[...], rows_ps[...], precision=HIGHEST, preferred_element_type=F32)
        w_high[...], w_low[...] = halve(
            lax.dot_general(
                work[...], half, (((0,), (0,)), ((), ())), precision=HIGHEST, preferred_element_type=F32
            )
        )

    def dot(a, b):
        return jnp.dot(a, b, preferred_element_type=F32)

    def update_rows():
        tiles = STEP // 128

        def step(i, carry):
            for j in range(tiles):
                lanes = pl.ds(pl.multiple_of(i * STEP + 128 * j, 128), 128)
                for c in range(NC):
                    part = slice(STRIP * c, STRIP * c + STRIP)
                    rows_t[part, 128 * j:128 * j + 128] = (
                        code[part, lanes].astype(jnp.int32).astype(F32) * scale[c, pl.ds(tiles * i + j, 1), :]
                    )
            here = pl.ds(pl.multiple_of(i * STEP, STEP), STEP)
            high, low = halve(rows_t[...])
            factor[:, here] = dot(own_high[...], high) + dot(own_high[...], low) + dot(own_low[...], high)
            high, low = high.T, low.T
            update = dot(high, w_high[...]) + dot(low, w_high[...]) + dot(high, w_low[...])
            keep = (row * (ROWS // STEP) + i) >= PANEL // STEP
            slab[here, :] = slab[here, :] - jnp.where(keep, update, 0.0)
            return carry

        lax.fori_loop(0, ROWS // STEP, step, 0)

    columns_pack(0)
    code_panel()
    pl.semaphore_wait(barrier, 37)
    top_first()
    ps_first()
    columns_hop(0)
    slab_load.start()
    columns_pack(1)
    columns_hop(1)
    top_hop()
    columns_pack(2)
    columns_hop(2)
    ps_second()
    columns_pack(3)
    columns_hop(3)
    rows_hop(0)
    gather_first()
    top_swap()
    rows_hop(1)
    ps_third()
    factor_start()
    factor_step(0)
    gather_second()
    rows_hop(2)
    factor_step(1)
    rows_hop(3)
    gather_third()
    factor_step(2)
    factor_step(3)
    factor_end()
    weights()
    gather_end()
    slab_load.wait()
    update_rows()

    for s in range(NS):
        for dz, dk in line:
            k, from_z = (core + dk) % 2, (z + dz) % 4
            landed(arrived.at[k, from_z, s], c2_recv.at[s, from_z, k])
    for copy in sends:
        copy.wait_send()

    @pl.when(row == 0)
    def _():
        for n, d in enumerate(line_away):
            top_out(n, d).wait_send()

    for v, g in ps_pairs:
        @pl.when((row == g) & (col != v + 9 * g))
        def _():
            for args in ps_out(v, g):
                remote(*args).wait_send()

    @pl.when(row == root)
    def _():
        for n, d in from_root:
            for copy in ps_copies(n, d):
                copy.wait_send()

    @pl.when((core == root) & (z > 0))
    def _():
        for copy in ps_copies(3, (0, 1)):
            copy.wait_send()


def exchange(slots, panel, child_one, child_two, slab):
    vmem = pl.BlockSpec(memory_space=pltpu.VMEM)
    hbm = pl.BlockSpec(memory_space=pltpu.HBM)
    dma = pltpu.SemaphoreType.DMA
    return pl.pallas_call(
        exchange_kernel,
        out_shape=(
            jax.ShapeDtypeStruct((2, 4, NS, CAP, SUB, 128), BF16),
            jax.ShapeDtypeStruct((ROWS, WIDTH), F32),
            jax.ShapeDtypeStruct((STRIP, ROWS), F32),
        ),
        in_specs=[pl.BlockSpec(memory_space=pltpu.SMEM)] + [vmem] * 3 + [hbm],
        out_specs=(vmem,) * 3,
        scratch_shapes=[
            pltpu.VMEM((PANEL, ROWS), jnp.int16),
            pltpu.VMEM((NC, ROWS // 128, 128), F32),
            pltpu.VMEM((PANEL, WIDTH), BF16),
            pltpu.VMEM((PANEL, WIDTH), BF16),
            pltpu.VMEM((STRIP, PANEL), BF16),
            pltpu.VMEM((STRIP, PANEL), BF16),
            pltpu.VMEM((PANEL, STEP), F32),
            pltpu.VMEM((NS, 2, NC, SUB, 128), BF16),
            pltpu.VMEM((NS, NC, 2, SUB, 128), BF16),
            pltpu.VMEM((NS, 2 * NC, SUB, 128), BF16),
            pltpu.VMEM((NS, NR, CAP, SUB, 128), BF16),
            pltpu.VMEM((STRIP, ROWS), jnp.int16),
            pltpu.VMEM((ROWS // 128, 128), F32),
            pltpu.VMEM((ROWS // PANEL, 8, 128), F32),
            pltpu.VMEM((PANEL, PANEL), F32),
            pltpu.VMEM((PANEL, WIDTH), jnp.int16),
            pltpu.VMEM((NC, 8, 128), F32),
            pltpu.VMEM((PANEL, PANEL), F32),
            pltpu.VMEM((128, 128), F32),
            pltpu.VMEM((PANEL, WIDTH), F32),
            dma(()),
            dma((23,)), dma(()), dma((NC,)), dma(()),
            dma((NS, NC, 2)), dma((NS, NC, 2)),
            dma((NS, NR)), dma((NS, 4, 2)),
            dma((2, 19)), dma((2, NC)), dma((2, 4, 2)),
            dma((15,)), dma((NC,)),
            dma((2, 9)), dma((2, NC)),
            dma((2, 4)), dma((2,)),
        ],
        compiler_params=pltpu.CompilerParams(
            collective_id=0, has_side_effects=True, vmem_limit_bytes=36 * 1024 * 1024
        ),
    )(slots, panel, child_one, child_two, slab)


def place_kernel(where, has, slab, factor, arrived, out, factor_out):
    i = pl.program_id(0)
    factor_out[...] = factor[...]
    for n in range(STEP // BLK):
        block = i * (STEP // BLK) + n
        one_at, two_at = where[block], where[ROWS // BLK + block]
        one_in, two_in = has[block] > 0, has[ROWS // BLK + block] > 0
        for s in range(NS):
            rows = slice(BLK * n + SUB * s, BLK * n + SUB * s + SUB)
            here = pl.ds(pl.multiple_of(i * STEP + BLK * n + SUB * s, SUB), SUB)
            for a in range(4):
                lanes = slice(128 * a, 128 * a + 128)
                one = jnp.where(one_in, arrived[0, a, s, one_at].astype(F32), 0.0)
                two = jnp.where(two_in, arrived[1, a, s, two_at].astype(F32), 0.0)
                out[rows, lanes] = (slab[here, lanes] + one) + two


def place(where, has, slab, factor, arrived):
    vmem = pl.BlockSpec(memory_space=pltpu.VMEM)
    part = pl.BlockSpec((STRIP, STEP), lambda i, w, h: (0, i))
    return pl.pallas_call(
        place_kernel,
        grid_spec=pltpu.PrefetchScalarGridSpec(
            num_scalar_prefetch=2,
            grid=(ROWS // STEP,),
            in_specs=[vmem, part, vmem],
            out_specs=[pl.BlockSpec((STEP, WIDTH), lambda i, w, h: (i, 0)), part],
        ),
        out_shape=(
            jax.ShapeDtypeStruct((ROWS, WIDTH), F32),
            jax.ShapeDtypeStruct((STRIP, ROWS), F32),
        ),
        compiler_params=pltpu.CompilerParams(vmem_limit_bytes=16 * 1024 * 1024),
    )(where, has, slab, factor, arrived)


def routing(maps):
    steps = ROWS // BLK
    owner = maps // steps
    count = maps.shape[1]
    before = jnp.arange(count)[None, :] < jnp.arange(count)[:, None]
    same = owner[:, :, None] == owner[:, None, :]
    rank = jnp.sum((same & before[None]).astype(jnp.int32), 2)
    slot = owner * CAP + rank
    hit = slot[:, None, :] == jnp.arange(NR * CAP)[None, :, None]
    slots = jnp.sum(jnp.where(hit, jnp.arange(count)[None, None, :], 0), 2)
    mine = lax.axis_index("row") * steps + jnp.arange(steps)
    at = maps[:, None, :] == mine[None, :, None]
    where = jnp.sum(jnp.where(at, rank[:, None, :], 0), 2)
    has = jnp.sum(at.astype(jnp.int32), 2)
    return tuple(v.reshape(-1).astype(jnp.int32) for v in (slots, where, has))


def per_device(front_panel, front_slab, child_one, child_two, map_one, map_two):
    slots, where, has = routing(jnp.stack([map_one, map_two]))
    arrived, slab, factor = exchange(slots, front_panel.T, child_one, child_two, front_slab)
    slab, factor = place(where, has, slab, factor, arrived)
    return (factor.T, slab)


def solution(mesh):
    in_specs = (P("row", "col"), P("row", "col"), P("col", "row"), P("col", "row"), P(), P())
    out_specs = (P("row", "col"), P("row", "col"))
    return jax.shard_map(
        per_device, mesh=mesh, in_specs=in_specs, out_specs=out_specs, check_vma=False
    )
```
